32 devices in a mesh: groups: 2 (over y), seq: 4 (over z), dp: 2 (over x), pair: 2 (over core).
Axes of the slice: x: 2, y: 2, z: 4, core: 2. Of those that a mesh axis runs over, the one named last changes fastest.
Arguments:
- queries: bfloat16 [4, 1024, 2048], P(('groups', 'dp'), ('seq', 'pair')), parts along dimension 0
- key_states: bfloat16 [4, 1024, 2048], P(('groups', 'dp'), ('seq', 'pair')), parts along dimension 0
- value_states: bfloat16 [4, 1024, 2048], P(('groups', 'dp'), ('seq', 'pair')), parts along dimension 0, may hold values from -6 to 6
- grad_output: bfloat16 [4, 1024, 2048], P(('groups', 'dp'), ('seq', 'pair')), parts along dimension 0
- gain_query: float32 [128], replicated, may hold values from 0.1 to 1.9
- gain_key: float32 [128], replicated, may hold values from 0.1 to 1.9
- block_keys: int32 [8, 4], replicated, may hold values from 0 to 7, as said below
- block_counts: int32 [8], replicated, may hold values from 1 to 128, as said below
Outputs:
- grad_query: bfloat16 [4, 1024, 2048], P(('groups', 'dp'), ('seq', 'pair')), parts along dimension 0
- grad_key: bfloat16 [4, 1024, 2048], P(('groups', 'dp'), ('seq', 'pair')), parts along dimension 0
- grad_value: bfloat16 [4, 1024, 2048], P(('groups', 'dp'), ('seq', 'pair')), parts along dimension 0
- grad_gain_query: float32 [256], P('groups'), parts along dimension 0
- grad_gain_key: float32 [256], P('groups'), parts along dimension 0
The draws below stay inside these ranges and needn't reach their ends.
There are 2 independent parts, one for each index of `groups`. The reference program is written for one: setup_inputs(seed, part) draws one part's arguments, and reference() takes and returns one part's arrays. A program takes and returns all parts, laid end to end along the dimension named above; an argument that names none is the same for every part. Nothing has to cross between parts.
Inputs may be any that keep to these rules, and one draw needn't show every extreme that they name: `block_keys`: each query block reads itself first, then three other blocks; the four are distinct. `block_counts`: some block is fully live and some block has one live position.
All inputs are finite; a program needn't handle non-finite values.
Results may differ from the reference program's by a relative error of at most 0.0087.
Values may be sent and summed in bfloat16 or wider, within the bound.
A program may use at most 128 MiB of HBM per device.

```python
import math
import jax
import jax.numpy as jnp
from jax import lax

H = 16
HD = 128
BLOCK = 128
KB = 4
D = 2048
SEQ = 1024
BATCH = 2
NB = 8


def rough_states(key):
    base_key, scale_key = jax.random.split(key, 2)
    row_scale = jnp.exp(jax.random.uniform(scale_key, (BATCH, SEQ, H, 1), jnp.float32, 0.0, math.log(10.0)))
    base = jax.random.normal(base_key, (BATCH, SEQ, H, HD), jnp.float32)
    return (base * row_scale).reshape(BATCH, SEQ, H * HD)


def draw_queries(key, part):
    return rough_states(jax.random.fold_in(key, 1)).astype(jnp.bfloat16)


def draw_key_states(key, part):
    return rough_states(jax.random.fold_in(key, 2)).astype(jnp.bfloat16)


def draw_grad_output(key, part):
    base_key = jax.random.fold_in(jax.random.fold_in(key, 3), 0)
    along = jnp.arange(SEQ, dtype=jnp.float32).reshape(1, SEQ, 1) / (SEQ - 1.0)
    across = jnp.arange(BATCH, dtype=jnp.float32).reshape(BATCH, 1, 1)
    rising = (1.0 + 2.0 * along) * (1.0 + 2.0 * across)
    base = jax.random.normal(base_key, (BATCH, SEQ, H * HD), jnp.float32)
    return (base * rising).astype(jnp.bfloat16)


def draw_block_keys(key, part):
    first_key, second_key, third_key = jax.random.split(jax.random.fold_in(key, 11), 3)
    third = NB // 3
    own = jnp.arange(NB, dtype=jnp.int32)
    offset_one = jax.random.randint(first_key, (NB,), 1, third, dtype=jnp.int32)
    offset_two = jax.random.randint(second_key, (NB,), third, 2 * third, dtype=jnp.int32)
    offset_three = jax.random.randint(third_key, (NB,), 2 * third, NB, dtype=jnp.int32)
    return jnp.stack([own, (own + offset_one) % NB, (own + offset_two) % NB, (own + offset_three) % NB], axis=1)


def draw_block_counts(key, part):
    count_key, pick_key = jax.random.split(jax.random.fold_in(key, 12), 2)
    counts = jax.random.randint(count_key, (NB,), 1, BLOCK + 1, dtype=jnp.int32)
    picked = jax.random.permutation(pick_key, NB)
    counts = counts.at[picked[0]].set(BLOCK)
    return counts.at[picked[1]].set(1)


def level_of(key, shape, pieces, least, high):
    def one(dim, shards_of):
        steps = jax.random.uniform(jax.random.fold_in(jax.random.fold_in(key, 6), dim), (shards_of,), jnp.float32, least / len(pieces), high / len(pieces))
        return jnp.repeat(jnp.exp(steps), shape[dim] // shards_of).reshape((-1,) + (1,) * (len(shape) - dim - 1))

    loudness = one(*pieces[0])
    for cut in pieces[1:]:
        loudness = loudness * one(*cut)
    return loudness


def normal_values(own_key, extent, deviation, reach, cuts=(), held_as=jnp.bfloat16):
    level = level_of(own_key, extent, cuts, -0.22, 0.18) if cuts else 1.0
    array = jax.random.normal(own_key, extent, jnp.float32) * deviation * level
    return jnp.minimum(jnp.maximum(array, -reach), reach).astype(held_as)


def setup_inputs(seed: int = 0, part: int = 0) -> dict:
    streams_of = jax.random.split(jax.random.key(seed), 9)
    part_keys = jax.random.split(jax.random.fold_in(streams_of[8], part), 9)
    queries = draw_queries(jax.random.fold_in(jax.random.fold_in(streams_of[8], part), 71), part)
    key_states = draw_key_states(jax.random.fold_in(jax.random.fold_in(streams_of[8], part), 71), part)
    value_states = normal_values(part_keys[2], (BATCH, SEQ, D), 1.0, 6.0, ((0, 2), (1, 8)))
    grad_output = draw_grad_output(jax.random.fold_in(jax.random.fold_in(streams_of[8], part), 71), part)
    gain_query = jnp.clip(1.0 + 0.18 * jax.random.normal(streams_of[4], (HD,), jnp.float32), 0.1, 1.9)
    gain_key = jnp.clip(1.0 + 0.18 * jax.random.normal(streams_of[5], (HD,), jnp.float32), 0.1, 1.9)
    block_keys = draw_block_keys(jax.random.fold_in(streams_of[8], 71), part)
    block_counts = draw_block_counts(jax.random.fold_in(streams_of[8], 71), part)
    return {"queries": queries, "key_states": key_states, "value_states": value_states, "grad_output": grad_output, "gain_query": gain_query, "gain_key": gain_key, "block_keys": block_keys, "block_counts": block_counts}


EPS = 1e-06

def head_grads(query_hat, key_hat, value_rows, grad_rows, block_keys, block_counts):
    score_scale = 1.0 / math.sqrt(HD)
    flat_keys = block_keys.reshape(-1).astype(jnp.int32)
    key_rows = jnp.take(key_hat, flat_keys, axis=0).reshape(NB, KB * BLOCK, HD).astype(jnp.float32)
    value_sel = jnp.take(value_rows, flat_keys, axis=0).reshape(NB, KB * BLOCK, HD).astype(jnp.float32)
    live_counts = jnp.take(block_counts, flat_keys).reshape(NB, KB, 1)
    live_mask = (lax.broadcasted_iota(jnp.int32, (NB, KB, BLOCK), 2) < live_counts).reshape(NB, 1, KB * BLOCK)
    query_float = query_hat.astype(jnp.float32)
    grad_float = grad_rows.astype(jnp.float32)
    scores = jnp.einsum('nqd,nkd->nqk', query_float, key_rows) * score_scale
    expd_scores = jnp.where(live_mask, jnp.exp(scores), 0.0)
    attn_probs = expd_scores / lax.optimization_barrier(jnp.sum(expd_scores, -1, keepdims=True))
    probs_low = lax.optimization_barrier(attn_probs.astype(jnp.bfloat16)).astype(jnp.float32)
    attended = jnp.einsum('nqk,nkd->nqd', probs_low, value_sel)
    delta_row = lax.optimization_barrier(jnp.sum(grad_float * attended, -1, keepdims=True))
    d_probs = jnp.einsum('nqd,nkd->nqk', grad_float, value_sel)
    d_scores = lax.optimization_barrier((attn_probs * (d_probs - delta_row) * score_scale).astype(jnp.bfloat16)).astype(jnp.float32)
    grad_query_hat = jnp.einsum('nqk,nkd->nqd', d_scores, key_rows).astype(jnp.bfloat16)
    key_terms = jnp.einsum('nqk,nqd->nkd', d_scores, query_float).reshape(NB * KB, BLOCK, HD)
    value_terms = jnp.einsum('nqk,nqd->nkd', probs_low, grad_float).reshape(NB * KB, BLOCK, HD)
    grad_key_hat = jnp.zeros((NB, BLOCK, HD), jnp.float32).at[flat_keys].add(key_terms).astype(jnp.bfloat16)
    grad_value = jnp.zeros((NB, BLOCK, HD), jnp.float32).at[flat_keys].add(value_terms).astype(jnp.bfloat16)
    return (grad_query_hat, grad_key_hat, grad_value)

def to_heads(states):
    return states.reshape(BATCH, NB, BLOCK, H, HD).transpose(0, 3, 1, 2, 4).reshape(BATCH * H, NB, BLOCK, HD)

def from_heads(states):
    return states.reshape(BATCH, H, NB, BLOCK, HD).transpose(0, 2, 3, 1, 4).reshape(BATCH, SEQ, H, HD)

def norm_backward(float_states, inverse, gain, grad_hat):
    grad_float = grad_hat.astype(jnp.float32)
    scaled = grad_float * gain
    inner = lax.optimization_barrier(jnp.mean(scaled * float_states, -1, keepdims=True))
    grad_states = inverse * scaled - float_states * inverse * inverse * inverse * inner
    return (grad_states, lax.optimization_barrier(jnp.sum(grad_float * float_states * inverse, axis=(0, 1, 2))))

def reference(queries, key_states, value_states, grad_output, gain_query, gain_key, block_keys, block_counts):
    query_float = queries.astype(jnp.float32).reshape(BATCH, SEQ, H, HD)
    key_float = key_states.astype(jnp.float32).reshape(BATCH, SEQ, H, HD)
    inv_query = lax.rsqrt(lax.optimization_barrier(jnp.mean(query_float * query_float, -1, keepdims=True)) + EPS)
    inv_key = lax.rsqrt(lax.optimization_barrier(jnp.mean(key_float * key_float, -1, keepdims=True)) + EPS)
    query_hat = (query_float * inv_query * gain_query).astype(jnp.bfloat16)
    key_hat = (key_float * inv_key * gain_key).astype(jnp.bfloat16)
    stacked = (to_heads(query_hat), to_heads(key_hat), to_heads(value_states.reshape(BATCH, SEQ, H, HD)), to_heads(grad_output.reshape(BATCH, SEQ, H, HD)))

    def per_head(items):
        return head_grads(items[0], items[1], items[2], items[3], block_keys, block_counts)
    grad_query_hat, grad_key_hat, grad_value = lax.map(per_head, stacked)
    grad_query_hat = from_heads(grad_query_hat)
    grad_key_hat = from_heads(grad_key_hat)
    grad_value = from_heads(grad_value)
    grad_query, gain_query_sum = norm_backward(query_float, inv_query, gain_query, grad_query_hat)
    grad_key, gain_key_sum = norm_backward(key_float, inv_key, gain_key, grad_key_hat)
    return (grad_query.astype(jnp.bfloat16).reshape(BATCH, SEQ, D), grad_key.astype(jnp.bfloat16).reshape(BATCH, SEQ, D), grad_value.reshape(BATCH, SEQ, D), gain_query_sum, gain_key_sum)
```

```python
import functools
import math

import jax
import jax.numpy as jnp
from jax import lax
from jax.experimental import pallas as pl
from jax.experimental.pallas import tpu as pltpu
from jax.sharding import PartitionSpec as P

BLOCK = 128


EPS = 1e-06


def normalize(states, gain):
    float_states = states.astype(jnp.float32)
    inverse = lax.rsqrt(jnp.mean(float_states * float_states, -1, keepdims=True) + EPS)
    return (float_states, inverse, (float_states * inverse * gain).astype(jnp.bfloat16))


def norm_backward(float_states, inverse, gain, grad_hat):
    grad_float = grad_hat.astype(jnp.float32)
    scaled = grad_float * gain
    inner = jnp.mean(scaled * float_states, -1, keepdims=True)
    grad_states = inverse * scaled - float_states * inverse * inverse * inverse * inner
    return (grad_states, jnp.sum(grad_float * float_states * inverse, axis=(0, 1)))


def to_items(states, row_parts):
    tokens, heads, head_dim = states.shape
    blocks_here = tokens // BLOCK
    shaped = states.reshape(blocks_here, row_parts, BLOCK // row_parts, heads, head_dim)
    return shaped.transpose(3, 1, 0, 2, 4).reshape(
        heads * row_parts, blocks_here, BLOCK // row_parts, head_dim
    )


def from_items(items, heads):
    total, blocks_here, piece_rows, head_dim = items.shape
    shaped = items.reshape(heads, total // heads, blocks_here, piece_rows, head_dim)
    return shaped.transpose(2, 1, 3, 0, 4).reshape(
        blocks_here * (total // heads) * piece_rows, heads, head_dim
    )


def key_copies(states, row_parts):
    tokens, heads, head_dim = states.shape
    shaped = states.reshape(tokens // BLOCK, BLOCK, heads, head_dim).transpose(2, 0, 1, 3)
    return jnp.repeat(shaped, row_parts, axis=0)


def fold_parts(items, heads):
    total, blocks_here, block_rows, head_dim = items.shape
    summed = jnp.sum(
        items.reshape(heads, total // heads, blocks_here, block_rows, head_dim), axis=1
    )
    return (
        summed.astype(jnp.bfloat16)
        .transpose(1, 2, 0, 3)
        .reshape(blocks_here * block_rows, heads, head_dim)
    )


def attend(query_items, grad_items, key_full, value_full, block_keys, block_counts):
    local_heads, total_blocks, piece_rows, head_dim = query_items.shape
    key_slots = block_keys.shape[1]
    group_blocks = max(1, min(total_blocks, 512 // piece_rows))
    while total_blocks % group_blocks:
        group_blocks = group_blocks // 2
    group_count = total_blocks // group_blocks
    score_scale = 1.0 / math.sqrt(head_dim)

    def one_group(turn, carry):
        grad_query, grad_keys, grad_values = carry
        head_at = turn // group_count
        first = turn % group_count * group_blocks
        query_block = lax.dynamic_slice(
            query_items, (head_at, first, 0, 0), (1, group_blocks, piece_rows, head_dim)
        )[0]
        grad_block = lax.dynamic_slice(
            grad_items, (head_at, first, 0, 0), (1, group_blocks, piece_rows, head_dim)
        )[0]
        chosen = lax.dynamic_slice_in_dim(block_keys, first, group_blocks, 0).reshape(-1)
        key_rows = jnp.take(lax.dynamic_index_in_dim(key_full, head_at, 0, False), chosen, axis=0)
        key_rows = key_rows.reshape(group_blocks, key_slots * BLOCK, head_dim)
        value_rows = jnp.take(
            lax.dynamic_index_in_dim(value_full, head_at, 0, False), chosen, axis=0
        )
        value_rows = value_rows.reshape(group_blocks, key_slots * BLOCK, head_dim)
        live_counts = jnp.take(block_counts, chosen).reshape(group_blocks, key_slots, 1)
        live_mask = (
            lax.broadcasted_iota(jnp.int32, (group_blocks, key_slots, BLOCK), 2) < live_counts
        )
        live_mask = live_mask.reshape(group_blocks, 1, key_slots * BLOCK)
        scores = (
            jnp.einsum("nqd,nkd->nqk", query_block, key_rows, preferred_element_type=jnp.float32)
            * score_scale
        )
        expd_scores = jnp.where(live_mask, jnp.exp(scores), 0.0)
        attn_probs = expd_scores / jnp.sum(expd_scores, -1, keepdims=True)
        probs_low = attn_probs.astype(jnp.bfloat16)
        attended = jnp.einsum(
            "nqk,nkd->nqd", probs_low, value_rows, preferred_element_type=jnp.float32
        )
        delta_row = jnp.sum(grad_block.astype(jnp.float32) * attended, -1, keepdims=True)
        d_probs = jnp.einsum(
            "nqd,nkd->nqk", grad_block, value_rows, preferred_element_type=jnp.float32
        )
        d_scores = (attn_probs * (d_probs - delta_row) * score_scale).astype(jnp.bfloat16)
        query_grad = jnp.einsum(
            "nqk,nkd->nqd", d_scores, key_rows, preferred_element_type=jnp.float32
        ).astype(jnp.bfloat16)
        key_terms = jnp.einsum(
            "nqk,nqd->nkd", d_scores, query_block, preferred_element_type=jnp.float32
        )
        value_terms = jnp.einsum(
            "nqk,nqd->nkd", probs_low, grad_block, preferred_element_type=jnp.float32
        )
        key_terms = key_terms.reshape(group_blocks * key_slots, BLOCK, head_dim)
        value_terms = value_terms.reshape(group_blocks * key_slots, BLOCK, head_dim)
        grad_query = lax.dynamic_update_slice(grad_query, query_grad[None], (head_at, first, 0, 0))
        grad_keys = grad_keys.at[head_at, chosen].add(key_terms)
        grad_values = grad_values.at[head_at, chosen].add(value_terms)
        return (grad_query, grad_keys, grad_values)

    initial = (
        jnp.zeros_like(query_items),
        jnp.zeros(key_full.shape, jnp.float32),
        jnp.zeros(value_full.shape, jnp.float32),
    )
    return lax.fori_loop(0, local_heads * group_count, one_group, initial)


def on_device(
    queries, key_states, value_states, grad_output, gain_query, gain_key, block_keys, block_counts
):
    tokens = queries.shape[1]
    head_dim = gain_query.shape[0]
    heads = queries.shape[2] // head_dim
    group_width = lax.axis_size(("seq", "pair"))
    row_parts = max(1, group_width // heads)
    query_float, query_inverse, query_hat = normalize(
        queries[0].reshape(tokens, heads, head_dim), gain_query
    )
    key_float, key_inverse, key_hat = normalize(
        key_states[0].reshape(tokens, heads, head_dim), gain_key
    )
    value_rows = value_states[0].reshape(tokens, heads, head_dim)
    grad_rows = grad_output[0].reshape(tokens, heads, head_dim)
    query_items, grad_items = (
        lax.all_to_all(
            to_items(query_hat, row_parts), ("seq", "pair"), split_axis=0, concat_axis=1, tiled=True
        ),
        lax.all_to_all(
            to_items(grad_rows, row_parts), ("seq", "pair"), split_axis=0, concat_axis=1, tiled=True
        ),
    )
    key_items, value_items = (
        lax.all_to_all(
            key_copies(key_hat, row_parts), ("seq", "pair"), split_axis=0, concat_axis=1, tiled=True
        ),
        lax.all_to_all(
            key_copies(value_rows, row_parts),
            ("seq", "pair"),
            split_axis=0,
            concat_axis=1,
            tiled=True,
        ),
    )
    grad_query_items, grad_keys, grad_values = attend(
        query_items, grad_items, key_items, value_items, block_keys, block_counts
    )
    back_query = lax.all_to_all(
        grad_query_items, ("seq", "pair"), split_axis=1, concat_axis=0, tiled=True
    )
    back_keys, back_values = (
        lax.all_to_all(
            grad_keys.astype(jnp.bfloat16), ("seq", "pair"), split_axis=1, concat_axis=0, tiled=True
        ).astype(grad_keys.dtype),
        lax.all_to_all(
            grad_values.astype(jnp.bfloat16),
            ("seq", "pair"),
            split_axis=1,
            concat_axis=0,
            tiled=True,
        ).astype(grad_values.dtype),
    )
    grad_query_hat = from_items(back_query, heads)
    grad_key_hat = fold_parts(back_keys, heads)
    grad_value_rows = fold_parts(back_values, heads)
    grad_query_rows, query_term = norm_backward(
        query_float, query_inverse, gain_query, grad_query_hat
    )
    grad_key_rows, key_term = norm_backward(key_float, key_inverse, gain_key, grad_key_hat)
    query_total, key_total = lax.psum((query_term, key_term), ("seq", "dp", "pair"))
    out_shape = queries.shape
    return (
        grad_query_rows.astype(jnp.bfloat16).reshape(out_shape),
        grad_key_rows.astype(jnp.bfloat16).reshape(out_shape),
        grad_value_rows.reshape(out_shape),
        query_total,
        key_total,
    )


MESH = pl.DeviceIdType.MESH
CHUNK = 256
LOG2E = 1.4426950408889634


def contract_last(left, right):
    return lax.dot_general(
        left, right, (((1,), (1,)), ((), ())), preferred_element_type=jnp.float32
    )


def contract(left, right):
    return jnp.dot(left, right, preferred_element_type=jnp.float32)


def fused_kernel(
    sizes,
    q_ref, k_ref, v_ref, g_ref, gain_q_ref, gain_k_ref, keys_ref, counts_ref,
    out_q, out_k, out_v, total_q, total_k,
    sent, held, bias, acc_k, acc_v, flipped, result, back, gains, gain_held,
    sent_send, sent_recv, result_send, result_recv, gain_send, gain_recv,
):
    pairs, group, replicas, local_heads = sizes
    tokens = q_ref.shape[0]
    seq_len = held.shape[2]
    total_blocks, slots = keys_ref.shape
    everyone = group * replicas
    me = lax.axis_index("seq") * pairs + lax.axis_index("pair")
    me_all = lax.axis_index("dp") * group + me

    def place(index):
        return {"seq": index // pairs, "pair": index % pairs}

    def place_all(index):
        inside = index % group
        return {"dp": index // group, "seq": inside // pairs, "pair": inside % pairs}

    def offset(turn):
        return group // 2 + ((turn + 1) // 2) * (1 - 2 * (turn % 2))

    barrier = pltpu.get_barrier_semaphore()
    for step in range(1, everyone):
        pl.semaphore_signal(
            barrier, inc=1, device_id=place_all((me_all + step) % everyone), device_id_type=MESH
        )
    gain_q = gain_q_ref[...]
    gain_k = gain_k_ref[...]

    def columns(head):
        return pl.ds(pl.multiple_of(head * 128, 128), 128)

    def rows(index):
        return pl.ds(pl.multiple_of(index * tokens, tokens), tokens)

    def inverse_of(states):
        return lax.rsqrt(jnp.mean(states * states, -1, keepdims=True) + EPS)

    def hat(states, gain):
        states = states.astype(jnp.float32)
        return (states * inverse_of(states) * gain).astype(jnp.bfloat16)

    def send_copy(local, turn):
        peer = (me + offset(turn)) % group
        return pltpu.make_async_remote_copy(
            src_ref=sent.at[local, peer],
            dst_ref=held.at[local, :, rows(me), :],
            send_sem=sent_send.at[local, turn],
            recv_sem=sent_recv.at[local, turn],
            device_id=place(peer),
            device_id_type=MESH,
        )

    def arrival(local, turn):
        source = (me + group - offset(turn)) % group
        return pltpu.make_async_remote_copy(
            src_ref=sent.at[local, source],
            dst_ref=held.at[local, :, rows(source), :],
            send_sem=sent_send.at[local, turn],
            recv_sem=sent_recv.at[local, turn],
            device_id=place(source),
            device_id_type=MESH,
        )

    def back_copy(local, turn):
        peer = (me + offset(turn)) % group
        return pltpu.make_async_remote_copy(
            src_ref=result.at[local, :, rows(peer), :],
            dst_ref=back.at[local, me],
            send_sem=result_send.at[local, turn],
            recv_sem=result_recv.at[local, turn],
            device_id=place(peer),
            device_id_type=MESH,
        )

    def back_arrival(local, turn):
        source = (me + group - offset(turn)) % group
        return pltpu.make_async_remote_copy(
            src_ref=result.at[local, :, rows(source), :],
            dst_ref=back.at[local, source],
            send_sem=result_send.at[local, turn],
            recv_sem=result_recv.at[local, turn],
            device_id=place(source),
            device_id_type=MESH,
        )

    for local in range(local_heads):

        def prepare(turn, carry, local=local):
            peer = (me + offset(turn)) % group
            at = columns(peer * local_heads + local)
            sent[local, peer, 0] = hat(q_ref[:, at], gain_q)
            sent[local, peer, 1] = hat(k_ref[:, at], gain_k)
            sent[local, peer, 2] = v_ref[:, at]
            sent[local, peer, 3] = g_ref[:, at]
            return carry

        def begin(turn, carry, local=local):
            carry = prepare(turn, carry, local)
            send_copy(local, turn).start()
            return carry

        if local == 0:
            prepare(0, 0)
            pl.semaphore_wait(barrier, everyone - 1)
            send_copy(0, 0).start()
            lax.fori_loop(1, group - 1, begin, 0)
        else:
            lax.fori_loop(0, group - 1, begin, 0)
    for local in range(local_heads):
        at = columns(me * local_heads + local)
        held[local, 0, rows(me), :] = hat(q_ref[:, at], gain_q)
        held[local, 1, rows(me), :] = hat(k_ref[:, at], gain_k)
        held[local, 2, rows(me), :] = v_ref[:, at]
        held[local, 3, rows(me), :] = g_ref[:, at]

    place_in = lax.broadcasted_iota(jnp.int32, (BLOCK, BLOCK), 0)
    for block in range(total_blocks):
        chunk, side = block // (CHUNK // BLOCK), block % (CHUNK // BLOCK)
        for other in range(total_blocks):
            live = counts_ref[other]
            limit = jnp.int32(0)
            for slot in range(slots):
                limit = jnp.where(keys_ref[block, slot] == other, live, limit)
            bias[
                chunk, other * BLOCK : (other + 1) * BLOCK, side * BLOCK : (side + 1) * BLOCK
            ] = jnp.where(place_in < limit, 0.0, -1e30)

    scale = 1.0 / math.sqrt(128)
    for local in range(local_heads):

        def landed(turn, carry, local=local):
            arrival(local, turn).wait_recv()
            return carry

        lax.fori_loop(0, group - 1, landed, 0)
        keys = held[local, 1]
        values = held[local, 2]
        flipped[0] = keys.T
        flipped[1] = values.T
        acc_k[...] = jnp.zeros_like(acc_k)
        acc_v[...] = jnp.zeros_like(acc_v)

        def one_chunk(chunk, carry, local=local):
            at = pl.ds(pl.multiple_of(chunk * CHUNK, CHUNK), CHUNK)
            query = held[local, 0, at, :]
            grad = held[local, 3, at, :]
            scores = contract_last(held[local, 1], query)
            expd = jnp.exp2(scores * (scale * LOG2E) + bias[chunk])
            probs = expd * (1.0 / jnp.sum(expd, 0, keepdims=True))
            probs_low = probs.astype(jnp.bfloat16)
            d_probs = contract_last(held[local, 2], grad)
            attended = contract(flipped[1], probs_low)
            delta = jnp.sum(grad.T.astype(jnp.float32) * attended, 0, keepdims=True)
            d_scores = (probs * ((d_probs - delta) * scale)).astype(jnp.bfloat16)
            grad_query = contract(flipped[0], d_scores)
            result[local, 0, at, :] = grad_query.T.astype(jnp.bfloat16)
            acc_k[...] += contract(d_scores, query)
            acc_v[...] += contract(probs_low, grad)
            return carry

        lax.fori_loop(0, seq_len // CHUNK, one_chunk, 0)
        result[local, 1] = acc_k[...].astype(jnp.bfloat16)
        result[local, 2] = acc_v[...].astype(jnp.bfloat16)

        def reply(turn, carry, local=local):
            back_copy(local, turn).start()
            return carry

        lax.fori_loop(0, group - 1, reply, 0)

    def finish(head, got_q, got_k, got_v, carry):
        at = columns(head)
        sums = []
        for ref, out, gain, got in ((q_ref, out_q, gain_q, got_q), (k_ref, out_k, gain_k, got_k)):
            states = ref[:, at].astype(jnp.float32)
            inverse = inverse_of(states)
            unit = states * inverse
            grad_hat = got.astype(jnp.float32)
            scaled = grad_hat * gain
            inner = jnp.mean(scaled * unit, -1, keepdims=True)
            out[:, at] = (inverse * (scaled - unit * inner)).astype(jnp.bfloat16)
            sums.append(jnp.sum((grad_hat * unit).reshape(tokens // 8, 8, 128), axis=0))
        out_v[:, at] = got_v
        return (carry[0] + sums[0], carry[1] + sums[1])

    nothing = jnp.zeros((8, 128), jnp.float32)
    terms = (nothing, nothing)
    for local in range(local_heads):
        terms = finish(
            me * local_heads + local,
            result[local, 0, rows(me), :],
            result[local, 1, rows(me), :],
            result[local, 2, rows(me), :],
            terms,
        )

        def collect(turn, carry, local=local):
            source = (me + group - offset(turn)) % group
            back_arrival(local, turn).wait_recv()
            return finish(
                source * local_heads + local,
                back[local, source, 0],
                back[local, source, 1],
                back[local, source, 2],
                carry,
            )

        terms = lax.fori_loop(0, group - 1, collect, terms)

    first = lax.broadcasted_iota(jnp.int32, (8, 128), 0) == 0
    both = jnp.where(
        first,
        jnp.sum(terms[0], 0, keepdims=True),
        jnp.sum(terms[1], 0, keepdims=True),
    )
    gains[...] = both
    gain_held[me_all] = both

    def gain_copy(step, sign):
        other = (me_all + everyone + sign * step) % everyone
        slot = me_all if sign > 0 else other
        return pltpu.make_async_remote_copy(
            src_ref=gains,
            dst_ref=gain_held.at[slot],
            send_sem=gain_send.at[step],
            recv_sem=gain_recv.at[step],
            device_id=place_all(other),
            device_id_type=MESH,
        )

    def gain_start(step, carry):
        gain_copy(step, 1).start()
        return carry

    def gain_wait(step, carry):
        gain_copy(step, -1).wait_recv()
        gain_copy(step, 1).wait_send()
        return carry

    lax.fori_loop(1, everyone, gain_start, 0)
    for local in range(local_heads):

        def drain(turn, carry, local=local):
            send_copy(local, turn).wait_send()
            back_copy(local, turn).wait_send()
            return carry

        lax.fori_loop(0, group - 1, drain, 0)
    lax.fori_loop(1, everyone, gain_wait, 0)
    summed = jnp.sum(gain_held[...], axis=0)
    total_q[...] = summed[0:1]
    total_k[...] = summed[1:2]


def on_device_fused(
    queries, key_states, value_states, grad_output, gain_query, gain_key, block_keys, block_counts
):
    tokens, features = queries.shape[1:]
    heads = features // gain_query.shape[0]
    group = lax.axis_size(("seq", "pair"))
    replicas = lax.axis_size("dp")
    local_heads = heads // group
    seq_len = tokens * group
    everyone = group * replicas
    low = jnp.bfloat16
    vmem = pl.BlockSpec(memory_space=pltpu.VMEM)
    smem = pl.BlockSpec(memory_space=pltpu.SMEM)
    shape = jax.ShapeDtypeStruct((tokens, features), low)
    line = jax.ShapeDtypeStruct((1, 128), jnp.float32)
    dma = pltpu.SemaphoreType.DMA
    outs = pl.pallas_call(
        functools.partial(
            fused_kernel, (lax.axis_size("pair"), group, replicas, local_heads)
        ),
        out_shape=(shape, shape, shape, line, line),
        in_specs=[vmem] * 6 + [smem] * 2,
        out_specs=(vmem,) * 5,
        scratch_shapes=[
            pltpu.VMEM((local_heads, group, 4, tokens, 128), low),
            pltpu.VMEM((local_heads, 4, seq_len, 128), low),
            pltpu.VMEM((seq_len // CHUNK, seq_len, CHUNK), jnp.float32),
            pltpu.VMEM((seq_len, 128), jnp.float32),
            pltpu.VMEM((seq_len, 128), jnp.float32),
            pltpu.VMEM((2, 128, seq_len), low),
            pltpu.VMEM((local_heads, 3, seq_len, 128), low),
            pltpu.VMEM((local_heads, group, 3, tokens, 128), low),
            pltpu.VMEM((8, 128), jnp.float32),
            pltpu.VMEM((everyone, 8, 128), jnp.float32),
            dma((local_heads, group)),
            dma((local_heads, group)),
            dma((local_heads, group)),
            dma((local_heads, group)),
            dma((everyone,)),
            dma((everyone,)),
        ],
        compiler_params=pltpu.CompilerParams(
            collective_id=0, has_side_effects=True, vmem_limit_bytes=56 * 1024 * 1024
        ),
    )(
        queries[0], key_states[0], value_states[0], grad_output[0],
        gain_query.reshape(1, 128), gain_key.reshape(1, 128), block_keys, block_counts,
    )
    return (
        outs[0][None], outs[1][None], outs[2][None], outs[3].reshape(128), outs[4].reshape(128)
    )


def on_device_any(*operands):
    queries, gain_query = operands[0], operands[4]
    tokens, features = queries.shape[1:]
    group = lax.axis_size(("seq", "pair"))
    heads = features // gain_query.shape[0]
    fits = group > 1 and group % 2 == 0 and heads % group == 0 and tokens % BLOCK == 0
    if fits and gain_query.shape[0] == 128 and tokens * group <= 1024:
        return on_device_fused(*operands)
    return on_device(*operands)


def solution(mesh):
    placed = (
        P(("groups", "dp"), ("seq", "pair"), None),
        P(("groups", "dp"), ("seq", "pair"), None),
        P(("groups", "dp"), ("seq", "pair"), None),
        P(("groups", "dp"), ("seq", "pair"), None),
        P(),
        P(),
        P(),
        P(),
    )
    return jax.shard_map(
        on_device_any,
        mesh=mesh,
        in_specs=placed,
        out_specs=(
            P(("groups", "dp"), ("seq", "pair"), None),
            P(("groups", "dp"), ("seq", "pair"), None),
            P(("groups", "dp"), ("seq", "pair"), None),
            P("groups"),
            P("groups"),
        ),
        check_vma=False,
    )
```

```python
import functools
import math

import jax
import jax.numpy as jnp
from jax import lax
from jax.experimental import pallas as pl
from jax.experimental.pallas import tpu as pltpu
from jax.sharding import PartitionSpec as P

BLOCK = 128


EPS = 1e-06


def normalize(states, gain):
    float_states = states.astype(jnp.float32)
    inverse = lax.rsqrt(jnp.mean(float_states * float_states, -1, keepdims=True) + EPS)
    return (float_states, inverse, (float_states * inverse * gain).astype(jnp.bfloat16))


def norm_backward(float_states, inverse, gain, grad_hat):
    grad_float = grad_hat.astype(jnp.float32)
    scaled = grad_float * gain
    inner = jnp.mean(scaled * float_states, -1, keepdims=True)
    grad_states = inverse * scaled - float_states * inverse * inverse * inverse * inner
    return (grad_states, jnp.sum(grad_float * float_states * inverse, axis=(0, 1)))


def to_items(states, row_parts):
    tokens, heads, head_dim = states.shape
    blocks_here = tokens // BLOCK
    shaped = states.reshape(blocks_here, row_parts, BLOCK // row_parts, heads, head_dim)
    return shaped.transpose(3, 1, 0, 2, 4).reshape(
        heads * row_parts, blocks_here, BLOCK // row_parts, head_dim
    )


def from_items(items, heads):
    total, blocks_here, piece_rows, head_dim = items.shape
    shaped = items.reshape(heads, total // heads, blocks_here, piece_rows, head_dim)
    return shaped.transpose(2, 1, 3, 0, 4).reshape(
        blocks_here * (total // heads) * piece_rows, heads, head_dim
    )


def key_copies(states, row_parts):
    tokens, heads, head_dim = states.shape
    shaped = states.reshape(tokens // BLOCK, BLOCK, heads, head_dim).transpose(2, 0, 1, 3)
    return jnp.repeat(shaped, row_parts, axis=0)


def fold_parts(items, heads):
    total, blocks_here, block_rows, head_dim = items.shape
    summed = jnp.sum(
        items.reshape(heads, total // heads, blocks_here, block_rows, head_dim), axis=1
    )
    return (
        summed.astype(jnp.bfloat16)
        .transpose(1, 2, 0, 3)
        .reshape(blocks_here * block_rows, heads, head_dim)
    )


def attend(query_items, grad_items, key_full, value_full, block_keys, block_counts):
    local_heads, total_blocks, piece_rows, head_dim = query_items.shape
    key_slots = block_keys.shape[1]
    group_blocks = max(1, min(total_blocks, 512 // piece_rows))
    while total_blocks % group_blocks:
        group_blocks = group_blocks // 2
    group_count = total_blocks // group_blocks
    score_scale = 1.0 / math.sqrt(head_dim)

    def one_group(turn, carry):
        grad_query, grad_keys, grad_values = carry
        head_at = turn // group_count
        first = turn % group_count * group_blocks
        query_block = lax.dynamic_slice(
            query_items, (head_at, first, 0, 0), (1, group_blocks, piece_rows, head_dim)
        )[0]
        grad_block = lax.dynamic_slice(
            grad_items, (head_at, first, 0, 0), (1, group_blocks, piece_rows, head_dim)
        )[0]
        chosen = lax.dynamic_slice_in_dim(block_keys, first, group_blocks, 0).reshape(-1)
        key_rows = jnp.take(lax.dynamic_index_in_dim(key_full, head_at, 0, False), chosen, axis=0)
        key_rows = key_rows.reshape(group_blocks, key_slots * BLOCK, head_dim)
        value_rows = jnp.take(
            lax.dynamic_index_in_dim(value_full, head_at, 0, False), chosen, axis=0
        )
        value_rows = value_rows.reshape(group_blocks, key_slots * BLOCK, head_dim)
        live_counts = jnp.take(block_counts, chosen).reshape(group_blocks, key_slots, 1)
        live_mask = (
            lax.broadcasted_iota(jnp.int32, (group_blocks, key_slots, BLOCK), 2) < live_counts
        )
        live_mask = live_mask.reshape(group_blocks, 1, key_slots * BLOCK)
        scores = (
            jnp.einsum("nqd,nkd->nqk", query_block, key_rows, preferred_element_type=jnp.float32)
            * score_scale
        )
        expd_scores = jnp.where(live_mask, jnp.exp(scores), 0.0)
        attn_probs = expd_scores / jnp.sum(expd_scores, -1, keepdims=True)
        probs_low = attn_probs.astype(jnp.bfloat16)
        attended = jnp.einsum(
            "nqk,nkd->nqd", probs_low, value_rows, preferred_element_type=jnp.float32
        )
        delta_row = jnp.sum(grad_block.astype(jnp.float32) * attended, -1, keepdims=True)
        d_probs = jnp.einsum(
            "nqd,nkd->nqk", grad_block, value_rows, preferred_element_type=jnp.float32
        )
        d_scores = (attn_probs * (d_probs - delta_row) * score_scale).astype(jnp.bfloat16)
        query_grad = jnp.einsum(
            "nqk,nkd->nqd", d_scores, key_rows, preferred_element_type=jnp.float32
        ).astype(jnp.bfloat16)
        key_terms = jnp.einsum(
            "nqk,nqd->nkd", d_scores, query_block, preferred_element_type=jnp.float32
        )
        value_terms = jnp.einsum(
            "nqk,nqd->nkd", probs_low, grad_block, preferred_element_type=jnp.float32
        )
        key_terms = key_terms.reshape(group_blocks * key_slots, BLOCK, head_dim)
        value_terms = value_terms.reshape(group_blocks * key_slots, BLOCK, head_dim)
        grad_query = lax.dynamic_update_slice(grad_query, query_grad[None], (head_at, first, 0, 0))
        grad_keys = grad_keys.at[head_at, chosen].add(key_terms)
        grad_values = grad_values.at[head_at, chosen].add(value_terms)
        return (grad_query, grad_keys, grad_values)

    initial = (
        jnp.zeros_like(query_items),
        jnp.zeros(key_full.shape, jnp.float32),
        jnp.zeros(value_full.shape, jnp.float32),
    )
    return lax.fori_loop(0, local_heads * group_count, one_group, initial)


def on_device(
    queries, key_states, value_states, grad_output, gain_query, gain_key, block_keys, block_counts
):
    tokens = queries.shape[1]
    head_dim = gain_query.shape[0]
    heads = queries.shape[2] // head_dim
    group_width = lax.axis_size(("seq", "pair"))
    row_parts = max(1, group_width // heads)
    query_float, query_inverse, query_hat = normalize(
        queries[0].reshape(tokens, heads, head_dim), gain_query
    )
    key_float, key_inverse, key_hat = normalize(
        key_states[0].reshape(tokens, heads, head_dim), gain_key
    )
    value_rows = value_states[0].reshape(tokens, heads, head_dim)
    grad_rows = grad_output[0].reshape(tokens, heads, head_dim)
    query_items, grad_items = (
        lax.all_to_all(
            to_items(query_hat, row_parts), ("seq", "pair"), split_axis=0, concat_axis=1, tiled=True
        ),
        lax.all_to_all(
            to_items(grad_rows, row_parts), ("seq", "pair"), split_axis=0, concat_axis=1, tiled=True
        ),
    )
    key_items, value_items = (
        lax.all_to_all(
            key_copies(key_hat, row_parts), ("seq", "pair"), split_axis=0, concat_axis=1, tiled=True
        ),
        lax.all_to_all(
            key_copies(value_rows, row_parts),
            ("seq", "pair"),
            split_axis=0,
            concat_axis=1,
            tiled=True,
        ),
    )
    grad_query_items, grad_keys, grad_values = attend(
        query_items, grad_items, key_items, value_items, block_keys, block_counts
    )
    back_query = lax.all_to_all(
        grad_query_items, ("seq", "pair"), split_axis=1, concat_axis=0, tiled=True
    )
    back_keys, back_values = (
        lax.all_to_all(
            grad_keys.astype(jnp.bfloat16), ("seq", "pair"), split_axis=1, concat_axis=0, tiled=True
        ).astype(grad_keys.dtype),
        lax.all_to_all(
            grad_values.astype(jnp.bfloat16),
            ("seq", "pair"),
            split_axis=1,
            concat_axis=0,
            tiled=True,
        ).astype(grad_values.dtype),
    )
    grad_query_hat = from_items(back_query, heads)
    grad_key_hat = fold_parts(back_keys, heads)
    grad_value_rows = fold_parts(back_values, heads)
    grad_query_rows, query_term = norm_backward(
        query_float, query_inverse, gain_query, grad_query_hat
    )
    grad_key_rows, key_term = norm_backward(key_float, key_inverse, gain_key, grad_key_hat)
    query_total, key_total = lax.psum((query_term, key_term), ("seq", "dp", "pair"))
    out_shape = queries.shape
    return (
        grad_query_rows.astype(jnp.bfloat16).reshape(out_shape),
        grad_key_rows.astype(jnp.bfloat16).reshape(out_shape),
        grad_value_rows.reshape(out_shape),
        query_total,
        key_total,
    )


MESH = pl.DeviceIdType.MESH
CHUNK = 256
LOG2E = 1.4426950408889634


def contract_last(left, right):
    return lax.dot_general(
        left, right, (((1,), (1,)), ((), ())), preferred_element_type=jnp.float32
    )


def contract(left, right):
    return jnp.dot(left, right, preferred_element_type=jnp.float32)


def fused_kernel(
    sizes,
    q_in, k_in, v_in, g_in, gain_q_ref, gain_k_ref, keys_in, counts_in,
    out_q, out_k, out_v, totals,
    q_ref, k_ref, v_ref, g_ref, keys_ref, counts_ref,
    sent, held, bias, acc_k, acc_v, flipped, result, back, gains, gain_held,
    sent_send, sent_recv, result_send, result_recv, gain_send, gain_recv, load_sem,
):
    pairs, group, replicas, local_heads = sizes
    tokens = q_ref.shape[0]
    seq_len = held.shape[2]
    slots, total_blocks = keys_ref.shape
    everyone = group * replicas
    me = lax.axis_index("seq") * pairs + lax.axis_index("pair")
    me_all = lax.axis_index("dp") * group + me

    def place(index):
        return {"seq": index // pairs, "pair": index % pairs}

    def place_all(index):
        inside = index % group
        return {"dp": index // group, "seq": inside // pairs, "pair": inside % pairs}

    def peer_of(turn):
        half = group // 2
        late = turn // half
        mask = (1 - late) * (half + turn) + late * (group - 1 - turn)
        peer, bit = 0, 1
        while bit < group:
            peer += ((me // bit + mask // bit) % 2) * bit
            bit *= 2
        return peer

    loads = [
        pltpu.make_async_copy(source, target, load_sem.at[at])
        for at, (source, target) in enumerate(
            (
                (q_in, q_ref), (k_in, k_ref), (v_in, v_ref), (g_in, g_ref),
                (keys_in, keys_ref), (counts_in, counts_ref),
            )
        )
    ]
    for load in loads:
        load.start()
    barrier = pltpu.get_barrier_semaphore()
    for step in range(1, everyone):
        pl.semaphore_signal(
            barrier, inc=1, device_id=place_all((me_all + step) % everyone), device_id_type=MESH
        )
    for load in loads:
        load.wait()
    gain_q = gain_q_ref[...]
    gain_k = gain_k_ref[...]

    def columns(head):
        return pl.ds(pl.multiple_of(head * 128, 128), 128)

    def rows(index):
        return pl.ds(pl.multiple_of(index * tokens, tokens), tokens)

    def inverse_of(states):
        return lax.rsqrt(jnp.mean(states * states, -1, keepdims=True) + EPS)

    def hat(states, gain):
        states = states.astype(jnp.float32)
        return (states * inverse_of(states) * gain).astype(jnp.bfloat16)

    def send_copy(local, turn):
        peer = peer_of(turn)
        return pltpu.make_async_remote_copy(
            src_ref=sent.at[local, peer],
            dst_ref=held.at[local, :, rows(me), :],
            send_sem=sent_send.at[local, turn],
            recv_sem=sent_recv.at[local, turn],
            device_id=place(peer),
            device_id_type=MESH,
        )

    def arrival(local, turn):
        source = peer_of(turn)
        return pltpu.make_async_remote_copy(
            src_ref=sent.at[local, source],
            dst_ref=held.at[local, :, rows(source), :],
            send_sem=sent_send.at[local, turn],
            recv_sem=sent_recv.at[local, turn],
            device_id=place(source),
            device_id_type=MESH,
        )

    def back_copy(local, turn):
        peer = peer_of(turn)
        return pltpu.make_async_remote_copy(
            src_ref=result.at[local, :, rows(peer), :],
            dst_ref=back.at[local, me],
            send_sem=result_send.at[local, turn],
            recv_sem=result_recv.at[local, turn],
            device_id=place(peer),
            device_id_type=MESH,
        )

    def back_arrival(local, turn):
        source = peer_of(turn)
        return pltpu.make_async_remote_copy(
            src_ref=result.at[local, :, rows(source), :],
            dst_ref=back.at[local, source],
            send_sem=result_send.at[local, turn],
            recv_sem=result_recv.at[local, turn],
            device_id=place(source),
            device_id_type=MESH,
        )

    for local in range(local_heads):

        def prepare(turn, carry, local=local):
            peer = peer_of(turn)
            at = columns(peer * local_heads + local)
            sent[local, peer, 0] = hat(q_ref[:, at], gain_q)
            sent[local, peer, 1] = hat(k_ref[:, at], gain_k)
            sent[local, peer, 2] = v_ref[:, at]
            sent[local, peer, 3] = g_ref[:, at]
            return carry

        def begin(turn, carry, local=local):
            carry = prepare(turn, carry, local)
            send_copy(local, turn).start()
            return carry

        if local == 0:
            prepare(0, 0)
            pl.semaphore_wait(barrier, everyone - 1)
            send_copy(0, 0).start()
            lax.fori_loop(1, group - 1, begin, 0)
        else:
            lax.fori_loop(0, group - 1, begin, 0)
    for local in range(local_heads):
        at = columns(me * local_heads + local)
        held[local, 0, rows(me), :] = hat(q_ref[:, at], gain_q)
        held[local, 1, rows(me), :] = hat(k_ref[:, at], gain_k)
        held[local, 2, rows(me), :] = v_ref[:, at]
        held[local, 3, rows(me), :] = g_ref[:, at]

    place_in = lax.broadcasted_iota(jnp.int32, (BLOCK, BLOCK), 0)
    for block in range(total_blocks):
        chunk, side = block // (CHUNK // BLOCK), block % (CHUNK // BLOCK)
        for other in range(total_blocks):
            live = counts_ref[0:1, other : other + 1]
            limit = jnp.zeros_like(live)
            for slot in range(slots):
                limit = jnp.where(keys_ref[slot : slot + 1, block : block + 1] == other, live, limit)
            bias[
                chunk, other * BLOCK : (other + 1) * BLOCK, side * BLOCK : (side + 1) * BLOCK
            ] = jnp.where(place_in < limit, 0.0, -1e30)

    scale = 1.0 / math.sqrt(128)
    gain_sums = [jnp.zeros((8, 128), jnp.float32), jnp.zeros((8, 128), jnp.float32)]
    for local in range(local_heads):

        def landed(turn, carry, local=local):
            arrival(local, turn).wait_recv()
            return carry

        lax.fori_loop(0, group - 1, landed, 0)
        keys = held[local, 1]
        values = held[local, 2]
        flipped[0] = keys.T
        flipped[1] = values.T
        acc_k[...] = jnp.zeros_like(acc_k)
        acc_v[...] = jnp.zeros_like(acc_v)

        def one_chunk(chunk, carry, local=local):
            at = pl.ds(pl.multiple_of(chunk * CHUNK, CHUNK), CHUNK)
            query = held[local, 0, at, :]
            grad = held[local, 3, at, :]
            scores = contract_last(held[local, 1], query)
            expd = jnp.exp2(scores * (scale * LOG2E) + bias[chunk])
            probs = expd * (1.0 / jnp.sum(expd, 0, keepdims=True))
            probs_low = probs.astype(jnp.bfloat16)
            d_probs = contract_last(held[local, 2], grad)
            attended = contract(flipped[1], probs_low)
            delta = jnp.sum(grad.T.astype(jnp.float32) * attended, 0, keepdims=True)
            d_scores = (probs * ((d_probs - delta) * scale)).astype(jnp.bfloat16)
            grad_query = contract(flipped[0], d_scores)
            result[local, 0, at, :] = grad_query.T.astype(jnp.bfloat16)
            acc_k[...] += contract(d_scores, query)
            acc_v[...] += contract(probs_low, grad)
            return carry

        lax.fori_loop(0, seq_len // CHUNK, one_chunk, 0)
        result[local, 1] = acc_k[...].astype(jnp.bfloat16)
        result[local, 2] = acc_v[...].astype(jnp.bfloat16)

        def fold(at, carry, local=local):
            part = pl.ds(pl.multiple_of(at * BLOCK, BLOCK), BLOCK)
            return tuple(
                total
                + jnp.sum(
                    (
                        result[local, which, part, :].astype(jnp.float32)
                        * held[local, which, part, :].astype(jnp.float32)
                    ).reshape(BLOCK // 8, 8, 128),
                    axis=0,
                )
                for which, total in enumerate(carry)
            )

        def reply(turn, carry, local=local):
            back_copy(local, turn).start()
            return carry

        lax.fori_loop(0, group - 1, reply, 0)
        gain_sums = lax.fori_loop(0, total_blocks, fold, tuple(gain_sums))

    first = lax.broadcasted_iota(jnp.int32, (8, 128), 0) == 0
    both = jnp.where(
        first,
        jnp.sum(gain_sums[0], 0, keepdims=True) / gain_q,
        jnp.sum(gain_sums[1], 0, keepdims=True) / gain_k,
    )
    gains[...] = both
    gain_held[me_all] = both

    def gain_copy(step, sign):
        other = (me_all + everyone + sign * step) % everyone
        slot = me_all if sign > 0 else other
        return pltpu.make_async_remote_copy(
            src_ref=gains,
            dst_ref=gain_held.at[slot],
            send_sem=gain_send.at[step],
            recv_sem=gain_recv.at[step],
            device_id=place_all(other),
            device_id_type=MESH,
        )

    def gain_start(step, carry):
        gain_copy(step, 1).start()
        return carry

    def gain_wait(step, carry):
        gain_copy(step, -1).wait_recv()
        gain_copy(step, 1).wait_send()
        return carry

    lax.fori_loop(1, everyone, gain_start, 0)

    def finish(head, got_q, got_k, got_v):
        at = columns(head)
        for ref, out, gain, got in ((q_ref, out_q, gain_q, got_q), (k_ref, out_k, gain_k, got_k)):
            states = ref[:, at].astype(jnp.float32)
            inverse = inverse_of(states)
            unit = states * inverse
            grad_hat = got.astype(jnp.float32)
            scaled = grad_hat * gain
            inner = jnp.mean(scaled * unit, -1, keepdims=True)
            out[:, at] = (inverse * (scaled - unit * inner)).astype(jnp.bfloat16)
        out_v[:, at] = got_v

    for local in range(local_heads):
        finish(
            me * local_heads + local,
            result[local, 0, rows(me), :],
            result[local, 1, rows(me), :],
            result[local, 2, rows(me), :],
        )

        def collect(turn, carry, local=local):
            source = peer_of(turn)
            back_arrival(local, turn).wait_recv()
            finish(
                source * local_heads + local,
                back[local, source, 0],
                back[local, source, 1],
                back[local, source, 2],
            )
            return carry

        lax.fori_loop(0, group - 1, collect, 0)

    for local in range(local_heads):

        def drain(turn, carry, local=local):
            send_copy(local, turn).wait_send()
            back_copy(local, turn).wait_send()
            return carry

        lax.fori_loop(0, group - 1, drain, 0)
    lax.fori_loop(1, everyone, gain_wait, 0)
    totals[...] = jnp.sum(gain_held[...], axis=0)


def place_kernel(
    a_in, b_in, c_in, totals, a_out, b_out, c_out, total_q, total_k, a_mid, b_mid, c_mid, sem
):
    steps = ((a_in, a_mid, a_out), (b_in, b_mid, b_out), (c_in, c_mid, c_out))
    first = [pltpu.make_async_copy(i, m, sem.at[0, at]) for at, (i, m, _) in enumerate(steps)]
    second = [pltpu.make_async_copy(m, o, sem.at[1, at]) for at, (_, m, o) in enumerate(steps)]
    for move in first:
        move.start()
    total_q[...] = totals[0:1]
    total_k[...] = totals[1:2]
    for before, after in zip(first, second):
        before.wait()
        after.start()
    for move in second:
        move.wait()


def on_device_fused(
    queries, key_states, value_states, grad_output, gain_query, gain_key, block_keys, block_counts
):
    tokens, features = queries.shape[1:]
    heads = features // gain_query.shape[0]
    group = lax.axis_size(("seq", "pair"))
    replicas = lax.axis_size("dp")
    local_heads = heads // group
    seq_len = tokens * group
    everyone = group * replicas
    low = jnp.bfloat16
    vmem = pl.BlockSpec(memory_space=pltpu.VMEM)
    hbm = pl.BlockSpec(memory_space=pl.ANY)
    shape = jax.ShapeDtypeStruct((tokens, features), low)
    line = jax.ShapeDtypeStruct((1, 128), jnp.float32)
    dma = pltpu.SemaphoreType.DMA
    outs = pl.pallas_call(
        functools.partial(
            fused_kernel, (lax.axis_size("pair"), group, replicas, local_heads)
        ),
        out_shape=(shape, shape, shape, jax.ShapeDtypeStruct((8, 128), jnp.float32)),
        in_specs=[hbm] * 4 + [vmem] * 2 + [hbm] * 2,
        out_specs=(vmem,) * 4,
        scratch_shapes=[
            pltpu.VMEM((tokens, features), low),
            pltpu.VMEM((tokens, features), low),
            pltpu.VMEM((tokens, features), low),
            pltpu.VMEM((tokens, features), low),
            pltpu.VMEM(block_keys.shape[::-1], block_keys.dtype),
            pltpu.VMEM((1, block_counts.shape[0]), block_counts.dtype),
            pltpu.VMEM((local_heads, group, 4, tokens, 128), low),
            pltpu.VMEM((local_heads, 4, seq_len, 128), low),
            pltpu.VMEM((seq_len // CHUNK, seq_len, CHUNK), jnp.float32),
            pltpu.VMEM((seq_len, 128), jnp.float32),
            pltpu.VMEM((seq_len, 128), jnp.float32),
            pltpu.VMEM((2, 128, seq_len), low),
            pltpu.VMEM((local_heads, 3, seq_len, 128), low),
            pltpu.VMEM((local_heads, group, 3, tokens, 128), low),
            pltpu.VMEM((8, 128), jnp.float32),
            pltpu.VMEM((everyone, 8, 128), jnp.float32),
            dma((local_heads, group)),
            dma((local_heads, group)),
            dma((local_heads, group)),
            dma((local_heads, group)),
            dma((everyone,)),
            dma((everyone,)),
            dma((6,)),
        ],
        compiler_params=pltpu.CompilerParams(
            collective_id=0, has_side_effects=True, vmem_limit_bytes=56 * 1024 * 1024
        ),
    )(
        queries[0], key_states[0], value_states[0], grad_output[0],
        gain_query.reshape(1, 128), gain_key.reshape(1, 128), block_keys.T, block_counts.reshape(1, -1),
    )
    outs = pl.pallas_call(
        place_kernel,
        out_shape=(shape, shape, shape, line, line),
        in_specs=[hbm] * 3 + [vmem],
        out_specs=(hbm,) * 3 + (vmem,) * 2,
        scratch_shapes=[pltpu.VMEM((tokens, features), low)] * 3 + [dma((2, 3))],
    )(*outs)
    return (
        outs[0][None], outs[1][None], outs[2][None], outs[3].reshape(128), outs[4].reshape(128)
    )


def on_device_any(*operands):
    queries, gain_query = operands[0], operands[4]
    tokens, features = queries.shape[1:]
    group = lax.axis_size(("seq", "pair"))
    heads = features // gain_query.shape[0]
    fits = group > 1 and group % 2 == 0 and heads % group == 0 and tokens % BLOCK == 0
    if fits and gain_query.shape[0] == 128 and tokens * group <= 1024:
        return on_device_fused(*operands)
    return on_device(*operands)


def solution(mesh):
    placed = (
        P(("groups", "dp"), ("seq", "pair"), None),
        P(("groups", "dp"), ("seq", "pair"), None),
        P(("groups", "dp"), ("seq", "pair"), None),
        P(("groups", "dp"), ("seq", "pair"), None),
        P(),
        P(),
        P(),
        P(),
    )
    return jax.shard_map(
        on_device_any,
        mesh=mesh,
        in_specs=placed,
        out_specs=(
            P(("groups", "dp"), ("seq", "pair"), None),
            P(("groups", "dp"), ("seq", "pair"), None),
            P(("groups", "dp"), ("seq", "pair"), None),
            P("groups"),
            P("groups"),
        ),
        check_vma=False,
    )
```

```python
import functools
import math

import jax
import jax.numpy as jnp
from jax import lax
from jax.experimental import pallas as pl
from jax.experimental.pallas import tpu as pltpu
from jax.sharding import PartitionSpec as P

BLOCK = 128


EPS = 1e-06


def normalize(states, gain):
    float_states = states.astype(jnp.float32)
    inverse = lax.rsqrt(jnp.mean(float_states * float_states, -1, keepdims=True) + EPS)
    return (float_states, inverse, (float_states * inverse * gain).astype(jnp.bfloat16))


def norm_backward(float_states, inverse, gain, grad_hat):
    grad_float = grad_hat.astype(jnp.float32)
    scaled = grad_float * gain
    inner = jnp.mean(scaled * float_states, -1, keepdims=True)
    grad_states = inverse * scaled - float_states * inverse * inverse * inverse * inner
    return (grad_states, jnp.sum(grad_float * float_states * inverse, axis=(0, 1)))


def to_items(states, row_parts):
    tokens, heads, head_dim = states.shape
    blocks_here = tokens // BLOCK
    shaped = states.reshape(blocks_here, row_parts, BLOCK // row_parts, heads, head_dim)
    return shaped.transpose(3, 1, 0, 2, 4).reshape(
        heads * row_parts, blocks_here, BLOCK // row_parts, head_dim
    )


def from_items(items, heads):
    total, blocks_here, piece_rows, head_dim = items.shape
    shaped = items.reshape(heads, total // heads, blocks_here, piece_rows, head_dim)
    return shaped.transpose(2, 1, 3, 0, 4).reshape(
        blocks_here * (total // heads) * piece_rows, heads, head_dim
    )


def key_copies(states, row_parts):
    tokens, heads, head_dim = states.shape
    shaped = states.reshape(tokens // BLOCK, BLOCK, heads, head_dim).transpose(2, 0, 1, 3)
    return jnp.repeat(shaped, row_parts, axis=0)


def fold_parts(items, heads):
    total, blocks_here, block_rows, head_dim = items.shape
    summed = jnp.sum(
        items.reshape(heads, total // heads, blocks_here, block_rows, head_dim), axis=1
    )
    return (
        summed.astype(jnp.bfloat16)
        .transpose(1, 2, 0, 3)
        .reshape(blocks_here * block_rows, heads, head_dim)
    )


def attend(query_items, grad_items, key_full, value_full, block_keys, block_counts):
    local_heads, total_blocks, piece_rows, head_dim = query_items.shape
    key_slots = block_keys.shape[1]
    group_blocks = max(1, min(total_blocks, 512 // piece_rows))
    while total_blocks % group_blocks:
        group_blocks = group_blocks // 2
    group_count = total_blocks // group_blocks
    score_scale = 1.0 / math.sqrt(head_dim)

    def one_group(turn, carry):
        grad_query, grad_keys, grad_values = carry
        head_at = turn // group_count
        first = turn % group_count * group_blocks
        query_block = lax.dynamic_slice(
            query_items, (head_at, first, 0, 0), (1, group_blocks, piece_rows, head_dim)
        )[0]
        grad_block = lax.dynamic_slice(
            grad_items, (head_at, first, 0, 0), (1, group_blocks, piece_rows, head_dim)
        )[0]
        chosen = lax.dynamic_slice_in_dim(block_keys, first, group_blocks, 0).reshape(-1)
        key_rows = jnp.take(lax.dynamic_index_in_dim(key_full, head_at, 0, False), chosen, axis=0)
        key_rows = key_rows.reshape(group_blocks, key_slots * BLOCK, head_dim)
        value_rows = jnp.take(
            lax.dynamic_index_in_dim(value_full, head_at, 0, False), chosen, axis=0
        )
        value_rows = value_rows.reshape(group_blocks, key_slots * BLOCK, head_dim)
        live_counts = jnp.take(block_counts, chosen).reshape(group_blocks, key_slots, 1)
        live_mask = (
            lax.broadcasted_iota(jnp.int32, (group_blocks, key_slots, BLOCK), 2) < live_counts
        )
        live_mask = live_mask.reshape(group_blocks, 1, key_slots * BLOCK)
        scores = (
            jnp.einsum("nqd,nkd->nqk", query_block, key_rows, preferred_element_type=jnp.float32)
            * score_scale
        )
        expd_scores = jnp.where(live_mask, jnp.exp(scores), 0.0)
        attn_probs = expd_scores / jnp.sum(expd_scores, -1, keepdims=True)
        probs_low = attn_probs.astype(jnp.bfloat16)
        attended = jnp.einsum(
            "nqk,nkd->nqd", probs_low, value_rows, preferred_element_type=jnp.float32
        )
        delta_row = jnp.sum(grad_block.astype(jnp.float32) * attended, -1, keepdims=True)
        d_probs = jnp.einsum(
            "nqd,nkd->nqk", grad_block, value_rows, preferred_element_type=jnp.float32
        )
        d_scores = (attn_probs * (d_probs - delta_row) * score_scale).astype(jnp.bfloat16)
        query_grad = jnp.einsum(
            "nqk,nkd->nqd", d_scores, key_rows, preferred_element_type=jnp.float32
        ).astype(jnp.bfloat16)
        key_terms = jnp.einsum(
            "nqk,nqd->nkd", d_scores, query_block, preferred_element_type=jnp.float32
        )
        value_terms = jnp.einsum(
            "nqk,nqd->nkd", probs_low, grad_block, preferred_element_type=jnp.float32
        )
        key_terms = key_terms.reshape(group_blocks * key_slots, BLOCK, head_dim)
        value_terms = value_terms.reshape(group_blocks * key_slots, BLOCK, head_dim)
        grad_query = lax.dynamic_update_slice(grad_query, query_grad[None], (head_at, first, 0, 0))
        grad_keys = grad_keys.at[head_at, chosen].add(key_terms)
        grad_values = grad_values.at[head_at, chosen].add(value_terms)
        return (grad_query, grad_keys, grad_values)

    initial = (
        jnp.zeros_like(query_items),
        jnp.zeros(key_full.shape, jnp.float32),
        jnp.zeros(value_full.shape, jnp.float32),
    )
    return lax.fori_loop(0, local_heads * group_count, one_group, initial)


def on_device(
    queries, key_states, value_states, grad_output, gain_query, gain_key, block_keys, block_counts
):
    tokens = queries.shape[1]
    head_dim = gain_query.shape[0]
    heads = queries.shape[2] // head_dim
    group_width = lax.axis_size(("seq", "pair"))
    row_parts = max(1, group_width // heads)
    query_float, query_inverse, query_hat = normalize(
        queries[0].reshape(tokens, heads, head_dim), gain_query
    )
    key_float, key_inverse, key_hat = normalize(
        key_states[0].reshape(tokens, heads, head_dim), gain_key
    )
    value_rows = value_states[0].reshape(tokens, heads, head_dim)
    grad_rows = grad_output[0].reshape(tokens, heads, head_dim)
    query_items, grad_items = (
        lax.all_to_all(
            to_items(query_hat, row_parts), ("seq", "pair"), split_axis=0, concat_axis=1, tiled=True
        ),
        lax.all_to_all(
            to_items(grad_rows, row_parts), ("seq", "pair"), split_axis=0, concat_axis=1, tiled=True
        ),
    )
    key_items, value_items = (
        lax.all_to_all(
            key_copies(key_hat, row_parts), ("seq", "pair"), split_axis=0, concat_axis=1, tiled=True
        ),
        lax.all_to_all(
            key_copies(value_rows, row_parts),
            ("seq", "pair"),
            split_axis=0,
            concat_axis=1,
            tiled=True,
        ),
    )
    grad_query_items, grad_keys, grad_values = attend(
        query_items, grad_items, key_items, value_items, block_keys, block_counts
    )
    back_query = lax.all_to_all(
        grad_query_items, ("seq", "pair"), split_axis=1, concat_axis=0, tiled=True
    )
    back_keys, back_values = (
        lax.all_to_all(
            grad_keys.astype(jnp.bfloat16), ("seq", "pair"), split_axis=1, concat_axis=0, tiled=True
        ).astype(grad_keys.dtype),
        lax.all_to_all(
            grad_values.astype(jnp.bfloat16),
            ("seq", "pair"),
            split_axis=1,
            concat_axis=0,
            tiled=True,
        ).astype(grad_values.dtype),
    )
    grad_query_hat = from_items(back_query, heads)
    grad_key_hat = fold_parts(back_keys, heads)
    grad_value_rows = fold_parts(back_values, heads)
    grad_query_rows, query_term = norm_backward(
        query_float, query_inverse, gain_query, grad_query_hat
    )
    grad_key_rows, key_term = norm_backward(key_float, key_inverse, gain_key, grad_key_hat)
    query_total, key_total = lax.psum((query_term, key_term), ("seq", "dp", "pair"))
    out_shape = queries.shape
    return (
        grad_query_rows.astype(jnp.bfloat16).reshape(out_shape),
        grad_key_rows.astype(jnp.bfloat16).reshape(out_shape),
        grad_value_rows.reshape(out_shape),
        query_total,
        key_total,
    )


MESH = pl.DeviceIdType.MESH
CHUNK = 256
LOG2E = 1.4426950408889634


def contract_last(left, right):
    return lax.dot_general(
        left, right, (((1,), (1,)), ((), ())), preferred_element_type=jnp.float32
    )


def contract(left, right):
    return jnp.dot(left, right, preferred_element_type=jnp.float32)


def fused_kernel(
    sizes,
    q_in, k_in, v_in, g_in, gain_q_ref, gain_k_ref, keys_in, counts_in,
    out_q, out_k, out_v, totals,
    q_ref, k_ref, v_ref, g_ref, keys_ref, counts_ref, units, inverses,
    sent, held, bias, acc_k, acc_v, flipped, result, back, gains, gain_held,
    sent_send, sent_recv, result_send, result_recv, gain_send, gain_recv, load_sem,
):
    pairs, group, replicas, local_heads = sizes
    tokens = q_ref.shape[0]
    seq_len = held.shape[2]
    slots, total_blocks = keys_ref.shape
    everyone = group * replicas
    me = lax.axis_index("seq") * pairs + lax.axis_index("pair")
    me_all = lax.axis_index("dp") * group + me

    def place(index):
        return {"seq": index // pairs, "pair": index % pairs}

    def place_all(index):
        inside = index % group
        return {"dp": index // group, "seq": inside // pairs, "pair": inside % pairs}

    def peer_of(turn):
        half = group // 2
        late = turn // half
        mask = (1 - late) * (half + turn) + late * (group - 1 - turn)
        peer, bit = 0, 1
        while bit < group:
            peer += ((me // bit + mask // bit) % 2) * bit
            bit *= 2
        return peer

    loads = [
        pltpu.make_async_copy(source, target, load_sem.at[at])
        for at, (source, target) in enumerate(
            (
                (q_in, q_ref), (k_in, k_ref), (v_in, v_ref), (g_in, g_ref),
                (keys_in, keys_ref), (counts_in, counts_ref),
            )
        )
    ]
    for load in loads:
        load.start()
    barrier = pltpu.get_barrier_semaphore()
    for step in range(1, everyone):
        pl.semaphore_signal(
            barrier, inc=1, device_id=place_all((me_all + step) % everyone), device_id_type=MESH
        )
    for load in loads:
        load.wait()
    gain_q = gain_q_ref[...]
    gain_k = gain_k_ref[...]

    def columns(head):
        return pl.ds(pl.multiple_of(head * 128, 128), 128)

    def rows(index):
        return pl.ds(pl.multiple_of(index * tokens, tokens), tokens)

    def inverse_of(states):
        return lax.rsqrt(jnp.mean(states * states, -1, keepdims=True) + EPS)

    def hat(states, gain):
        states = states.astype(jnp.float32)
        return (states * inverse_of(states) * gain).astype(jnp.bfloat16)

    def send_copy(local, turn):
        peer = peer_of(turn)
        return pltpu.make_async_remote_copy(
            src_ref=sent.at[local, peer],
            dst_ref=held.at[local, :, rows(me), :],
            send_sem=sent_send.at[local, turn],
            recv_sem=sent_recv.at[local, turn],
            device_id=place(peer),
            device_id_type=MESH,
        )

    def arrival(local, turn):
        source = peer_of(turn)
        return pltpu.make_async_remote_copy(
            src_ref=sent.at[local, source],
            dst_ref=held.at[local, :, rows(source), :],
            send_sem=sent_send.at[local, turn],
            recv_sem=sent_recv.at[local, turn],
            device_id=place(source),
            device_id_type=MESH,
        )

    def back_copy(local, turn):
        peer = peer_of(turn)
        return pltpu.make_async_remote_copy(
            src_ref=result.at[local, :, rows(peer), :],
            dst_ref=back.at[local, me],
            send_sem=result_send.at[local, turn],
            recv_sem=result_recv.at[local, turn],
            device_id=place(peer),
            device_id_type=MESH,
        )

    def back_arrival(local, turn):
        source = peer_of(turn)
        return pltpu.make_async_remote_copy(
            src_ref=result.at[local, :, rows(source), :],
            dst_ref=back.at[local, source],
            send_sem=result_send.at[local, turn],
            recv_sem=result_recv.at[local, turn],
            device_id=place(source),
            device_id_type=MESH,
        )

    for local in range(local_heads):

        def prepare(turn, carry, local=local):
            peer = peer_of(turn)
            at = columns(peer * local_heads + local)
            sent[local, peer, 0] = hat(q_ref[:, at], gain_q)
            sent[local, peer, 1] = hat(k_ref[:, at], gain_k)
            sent[local, peer, 2] = v_ref[:, at]
            sent[local, peer, 3] = g_ref[:, at]
            return carry

        def begin(turn, carry, local=local):
            carry = prepare(turn, carry, local)
            send_copy(local, turn).start()
            return carry

        if local == 0:
            prepare(0, 0)
            pl.semaphore_wait(barrier, everyone - 1)
            send_copy(0, 0).start()
            lax.fori_loop(1, group - 1, begin, 0)
        else:
            lax.fori_loop(0, group - 1, begin, 0)
    for local in range(local_heads):
        at = columns(me * local_heads + local)
        held[local, 0, rows(me), :] = hat(q_ref[:, at], gain_q)
        held[local, 1, rows(me), :] = hat(k_ref[:, at], gain_k)
        held[local, 2, rows(me), :] = v_ref[:, at]
        held[local, 3, rows(me), :] = g_ref[:, at]

    place_in = lax.broadcasted_iota(jnp.int32, (BLOCK, BLOCK), 0)
    for block in range(total_blocks):
        chunk, side = block // (CHUNK // BLOCK), block % (CHUNK // BLOCK)
        for other in range(total_blocks):
            live = counts_ref[0:1, other : other + 1]
            limit = jnp.zeros_like(live)
            for slot in range(slots):
                limit = jnp.where(keys_ref[slot : slot + 1, block : block + 1] == other, live, limit)
            bias[
                chunk, other * BLOCK : (other + 1) * BLOCK, side * BLOCK : (side + 1) * BLOCK
            ] = jnp.where(place_in < limit, 0.0, -1e30)

    def remember(head, carry):
        for which, ref in enumerate((q_ref, k_ref)):
            states = ref[:, columns(head)].astype(jnp.float32)
            inverse = inverse_of(states)
            units[which, head] = states * inverse
            inverses[which, head] = jnp.broadcast_to(inverse, states.shape)
        return carry

    lax.fori_loop(0, local_heads * group, remember, 0)
    def gain_copy(step, sign):
        other = (me_all + everyone + sign * step) % everyone
        slot = me_all if sign > 0 else other
        return pltpu.make_async_remote_copy(
            src_ref=gains,
            dst_ref=gain_held.at[slot],
            send_sem=gain_send.at[step],
            recv_sem=gain_recv.at[step],
            device_id=place_all(other),
            device_id_type=MESH,
        )

    def gain_start(step, carry):
        gain_copy(step, 1).start()
        return carry

    def gain_wait(step, carry):
        gain_copy(step, -1).wait_recv()
        gain_copy(step, 1).wait_send()
        return carry

    def share_gains(gain_sums):
        first = lax.broadcasted_iota(jnp.int32, (8, 128), 0) == 0
        both = jnp.where(
            first,
            jnp.sum(gain_sums[0], 0, keepdims=True) / gain_q,
            jnp.sum(gain_sums[1], 0, keepdims=True) / gain_k,
        )
        gains[...] = both
        gain_held[me_all] = both
        lax.fori_loop(1, everyone, gain_start, 0)

    scale = 1.0 / math.sqrt(128)
    gain_sums = [jnp.zeros((8, 128), jnp.float32), jnp.zeros((8, 128), jnp.float32)]
    for local in range(local_heads):

        def landed(turn, carry, local=local):
            arrival(local, turn).wait_recv()
            return carry

        lax.fori_loop(0, group - 1, landed, 0)
        keys = held[local, 1]
        values = held[local, 2]
        flipped[0] = keys.T
        flipped[1] = values.T
        acc_k[...] = jnp.zeros_like(acc_k)
        acc_v[...] = jnp.zeros_like(acc_v)

        def one_chunk(chunk, carry, local=local):
            at = pl.ds(pl.multiple_of(chunk * CHUNK, CHUNK), CHUNK)
            query = held[local, 0, at, :]
            grad = held[local, 3, at, :]
            scores = contract_last(held[local, 1], query)
            expd = jnp.exp2(scores * (scale * LOG2E) + bias[chunk])
            probs = expd * (1.0 / jnp.sum(expd, 0, keepdims=True))
            probs_low = probs.astype(jnp.bfloat16)
            d_probs = contract_last(held[local, 2], grad)
            attended = contract(flipped[1], probs_low)
            delta = jnp.sum(grad.T.astype(jnp.float32) * attended, 0, keepdims=True)
            d_scores = (probs * ((d_probs - delta) * scale)).astype(jnp.bfloat16)
            grad_query = contract(flipped[0], d_scores)
            result[local, 0, at, :] = grad_query.T.astype(jnp.bfloat16)
            acc_k[...] += contract(d_scores, query)
            acc_v[...] += contract(probs_low, grad)
            return carry

        lax.fori_loop(0, seq_len // CHUNK, one_chunk, 0)
        result[local, 1] = acc_k[...].astype(jnp.bfloat16)
        result[local, 2] = acc_v[...].astype(jnp.bfloat16)

        def fold(at, carry, local=local):
            part = pl.ds(pl.multiple_of(at * BLOCK, BLOCK), BLOCK)
            return tuple(
                total
                + jnp.sum(
                    (
                        result[local, which, part, :].astype(jnp.float32)
                        * held[local, which, part, :].astype(jnp.float32)
                    ).reshape(BLOCK // 8, 8, 128),
                    axis=0,
                )
                for which, total in enumerate(carry)
            )

        def reply(turn, carry, local=local):
            back_copy(local, turn).start()
            return carry

        gain_sums = lax.fori_loop(0, total_blocks, fold, tuple(gain_sums))
        if local == local_heads - 1:
            share_gains(gain_sums)
        lax.fori_loop(0, group - 1, reply, 0)

    def finish(head, got_q, got_k, got_v):
        at = columns(head)
        for which, (out, gain, got) in enumerate(((out_q, gain_q, got_q), (out_k, gain_k, got_k))):
            unit = units[which, head]
            inverse = inverses[which, head]
            grad_hat = got.astype(jnp.float32)
            scaled = grad_hat * gain
            inner = jnp.mean(scaled * unit, -1, keepdims=True)
            out[:, at] = (inverse * (scaled - unit * inner)).astype(jnp.bfloat16)
        out_v[:, at] = got_v

    for local in range(local_heads):
        finish(
            me * local_heads + local,
            result[local, 0, rows(me), :],
            result[local, 1, rows(me), :],
            result[local, 2, rows(me), :],
        )

        def drain(turn, carry, local=local):
            send_copy(local, turn).wait_send()
            return carry

        lax.fori_loop(0, group - 1, drain, 0)

        def collect(step, carry, local=local):
            turn = group - 2 - step
            source = peer_of(turn)
            back_arrival(local, turn).wait_recv()
            finish(
                source * local_heads + local,
                back[local, source, 0],
                back[local, source, 1],
                back[local, source, 2],
            )
            return carry

        if local == local_heads - 1:
            lax.fori_loop(1, everyone, gain_wait, 0)
            totals[...] = jnp.sum(gain_held[...], axis=0)
        lax.fori_loop(0, group - 1, collect, 0)

    for local in range(local_heads):

        def replied(turn, carry, local=local):
            back_copy(local, turn).wait_send()
            return carry

        lax.fori_loop(0, group - 1, replied, 0)


def place_kernel(
    a_in, b_in, c_in, totals, a_out, b_out, c_out, total_q, total_k, a_mid, b_mid, c_mid, sem
):
    steps = ((a_in, a_mid, a_out), (b_in, b_mid, b_out), (c_in, c_mid, c_out))
    first = [pltpu.make_async_copy(i, m, sem.at[0, at]) for at, (i, m, _) in enumerate(steps)]
    second = [pltpu.make_async_copy(m, o, sem.at[1, at]) for at, (_, m, o) in enumerate(steps)]
    for move in first:
        move.start()
    total_q[...] = totals[0:1]
    total_k[...] = totals[1:2]
    for before, after in zip(first, second):
        before.wait()
        after.start()
    for move in second:
        move.wait()


def on_device_fused(
    queries, key_states, value_states, grad_output, gain_query, gain_key, block_keys, block_counts
):
    tokens, features = queries.shape[1:]
    heads = features // gain_query.shape[0]
    group = lax.axis_size(("seq", "pair"))
    replicas = lax.axis_size("dp")
    local_heads = heads // group
    seq_len = tokens * group
    everyone = group * replicas
    low = jnp.bfloat16
    vmem = pl.BlockSpec(memory_space=pltpu.VMEM)
    hbm = pl.BlockSpec(memory_space=pl.ANY)
    shape = jax.ShapeDtypeStruct((tokens, features), low)
    line = jax.ShapeDtypeStruct((1, 128), jnp.float32)
    dma = pltpu.SemaphoreType.DMA
    outs = pl.pallas_call(
        functools.partial(
            fused_kernel, (lax.axis_size("pair"), group, replicas, local_heads)
        ),
        out_shape=(shape, shape, shape, jax.ShapeDtypeStruct((8, 128), jnp.float32)),
        in_specs=[hbm] * 4 + [vmem] * 2 + [hbm] * 2,
        out_specs=(vmem,) * 4,
        scratch_shapes=[
            pltpu.VMEM((tokens, features), low),
            pltpu.VMEM((tokens, features), low),
            pltpu.VMEM((tokens, features), low),
            pltpu.VMEM((tokens, features), low),
            pltpu.VMEM(block_keys.shape[::-1], block_keys.dtype),
            pltpu.VMEM((1, block_counts.shape[0]), block_counts.dtype),
            pltpu.VMEM((2, heads, tokens, 128), jnp.float32),
            pltpu.VMEM((2, heads, tokens, 128), jnp.float32),
            pltpu.VMEM((local_heads, group, 4, tokens, 128), low),
            pltpu.VMEM((local_heads, 4, seq_len, 128), low),
            pltpu.VMEM((seq_len // CHUNK, seq_len, CHUNK), jnp.float32),
            pltpu.VMEM((seq_len, 128), jnp.float32),
            pltpu.VMEM((seq_len, 128), jnp.float32),
            pltpu.VMEM((2, 128, seq_len), low),
            pltpu.VMEM((local_heads, 3, seq_len, 128), low),
            pltpu.VMEM((local_heads, group, 3, tokens, 128), low),
            pltpu.VMEM((8, 128), jnp.float32),
            pltpu.VMEM((everyone, 8, 128), jnp.float32),
            dma((local_heads, group)),
            dma((local_heads, group)),
            dma((local_heads, group)),
            dma((local_heads, group)),
            dma((everyone,)),
            dma((everyone,)),
            dma((6,)),
        ],
        compiler_params=pltpu.CompilerParams(
            collective_id=0, has_side_effects=True, vmem_limit_bytes=56 * 1024 * 1024
        ),
    )(
        queries[0], key_states[0], value_states[0], grad_output[0],
        gain_query.reshape(1, 128), gain_key.reshape(1, 128), block_keys.T, block_counts.reshape(1, -1),
    )
    outs = pl.pallas_call(
        place_kernel,
        out_shape=(shape, shape, shape, line, line),
        in_specs=[hbm] * 3 + [vmem],
        out_specs=(hbm,) * 3 + (vmem,) * 2,
        scratch_shapes=[pltpu.VMEM((tokens, features), low)] * 3 + [dma((2, 3))],
    )(*outs)
    return (
        outs[0][None], outs[1][None], outs[2][None], outs[3].reshape(128), outs[4].reshape(128)
    )


def on_device_any(*operands):
    queries, gain_query = operands[0], operands[4]
    tokens, features = queries.shape[1:]
    group = lax.axis_size(("seq", "pair"))
    heads = features // gain_query.shape[0]
    fits = group > 1 and group % 2 == 0 and heads % group == 0 and tokens % BLOCK == 0
    if fits and gain_query.shape[0] == 128 and tokens * group <= 1024:
        return on_device_fused(*operands)
    return on_device(*operands)


def solution(mesh):
    placed = (
        P(("groups", "dp"), ("seq", "pair"), None),
        P(("groups", "dp"), ("seq", "pair"), None),
        P(("groups", "dp"), ("seq", "pair"), None),
        P(("groups", "dp"), ("seq", "pair"), None),
        P(),
        P(),
        P(),
        P(),
    )
    return jax.shard_map(
        on_device_any,
        mesh=mesh,
        in_specs=placed,
        out_specs=(
            P(("groups", "dp"), ("seq", "pair"), None),
            P(("groups", "dp"), ("seq", "pair"), None),
            P(("groups", "dp"), ("seq", "pair"), None),
            P("groups"),
            P("groups"),
        ),
        check_vma=False,
    )
```
